32 devices in a mesh: section: 4 (over y, x), expert: 8 (over z, core).
Axes of the slice: x: 2, y: 2, z: 4, core: 2. Of those that a mesh axis runs over, the one named last changes fastest.
Arguments:
- forward_held: bfloat16 [4, 512, 3584], P('section', 'expert'), may hold values from -6 to 6
- forward_enter: bfloat16 [1, 512, 3584], P(None, 'expert'), may hold values from -6 to 6
- backward_held: bfloat16 [4, 512, 3584], P('section', 'expert'), may hold values from -6 to 6
- backward_enter: bfloat16 [1, 512, 3584], P(None, 'expert'), may hold values from -6 to 6
- stashed_inputs: bfloat16 [4, 2, 512, 3584], P('section', None, 'expert'), may hold values from -6 to 6
- gate_weight: bfloat16 [4, 16, 3584, 1024], P('section', 'expert'), may hold values from -0.09375 to 0.09375
- up_weight: bfloat16 [4, 16, 3584, 1024], P('section', 'expert'), may hold values from -0.09375 to 0.09375
- down_weight: bfloat16 [4, 16, 1024, 3584], P('section', 'expert'), may hold values from -0.1875 to 0.1875
- norm_gain: float32 [4, 3584], P('section'), may hold values from 0.5 to 2
- expert_ids: int32 [4, 4, 512, 2], P('section', None, 'expert'), may hold values from 0 to 15, all different within a row; in each aligned block of 64 rows (0 to 63, 64 to 127, ..., all dimensions but the last counted through in order) at most 12 rows name the same one
- router_scores: float32 [4, 4, 512, 2], P('section', None, 'expert'), may hold values from 0.02 to 1
Outputs:
- forward_out: bfloat16 [2, 4, 512, 3584], P(None, 'section', 'expert')
- backward_out: bfloat16 [2, 4, 512, 3584], P(None, 'section', 'expert')
The draws below stay inside these ranges and needn't reach their ends.
Inputs may be any that keep to these rules, and one draw needn't show every extreme that they name: `expert_ids`: each token names 2 different experts; in each section, micro-batch index and aligned block of 64 tokens no expert is named by more than 12 tokens.
All inputs are finite; a program needn't handle non-finite values.
Results may differ from the reference program's by a relative error of at most 0.0087.
Values may be sent and summed in bfloat16 or wider, within the bound.
A program may use at most 192 MiB of HBM per device.

```python
import math
import jax
import jax.numpy as jnp
import numpy as np
from jax import lax

D = 3584
FE = 1024
EXPERTS = 16
TOPK = 2
TICKS = 2
TOK_DEV = 64
CAP = 12
TOKENS = 512
N_SECTION = 4


def shard_levels(key, dims, split, low, top_value):
    def one(position, parts):
        heights = jax.random.uniform(jax.random.fold_in(jax.random.fold_in(key, 6), position), (parts,), jnp.float32, low / len(split), top_value / len(split))
        return jnp.repeat(jnp.exp(heights), dims[position] // parts).reshape((-1,) + (1,) * (len(dims) - position - 1))

    level = one(*split[0])
    for cut in split[1:]:
        level = level * one(*cut)
    return level


def routed_block(key, own, number, rows, count, top, most, skew):
    ranking = jax.random.permutation(key, count)
    heavy_load, usual = portions_of(count, rows * top, most, skew, True), portions_of(count, rows * top, most, skew, False)
    places = jnp.arange(count)

    def named(lengths, turn):
        used = int((lengths > 0).sum())
        fixed = max(1, used // 4)
        moved = fixed + (places - fixed + turn * (used - fixed)) % max(1, count - fixed)
        return jnp.zeros((count,), jnp.int32).at[ranking[jnp.where(places < fixed, places, moved)]].set(jnp.asarray(lengths, jnp.int32))

    lengths = jnp.where(number % 4 == 0, named(heavy_load, number // 4), named(usual, number - number // 4 - 1))
    mixed = jax.random.permutation(jax.random.fold_in(own, 3), count)
    donor, taker = mixed[0:count // 2 * 2:2], mixed[1:count // 2 * 2:2]
    room = jnp.minimum(lengths[donor] - 1, most - lengths[taker]) // 2
    room = jnp.where((donor == ranking[0]) | (taker == ranking[0]) | (lengths[taker] == 0), 0, jnp.maximum(room, 0))
    moved = jax.random.randint(jax.random.fold_in(own, 4), (count // 2,), 0, 1 << 20) % (room + 1)
    lengths = lengths.at[donor].add(-moved).at[taker].add(moved)
    members = jnp.searchsorted(jnp.cumsum(lengths), jnp.arange(rows * top), side="right").astype(jnp.int32)
    listing = members.reshape(top, rows).T
    listing = listing[jax.random.permutation(jax.random.fold_in(own, 1), rows)]
    turn = jax.random.randint(jax.random.fold_in(own, 2), (rows, 1), 0, top)
    return jnp.take_along_axis(listing, (jnp.arange(top)[None, :] + turn) % top, axis=1)


def portions_of(amount, total, most, lean, full):
    loads = [(1 << 20) // math.isqrt(standing ** lean) + 1 for standing in range(1, amount + 1)]
    largest = most if full else min(most, max(-(-total // amount), total * loads[0] // sum(loads)))
    least = 1 if total - largest >= amount - 1 else 0
    counts, spare = [largest] + [least] * (amount - 1), total - largest - least * (amount - 1)
    while spare > 0:
        free = [i for i in range(1, amount) if counts[i] < largest] or [i for i in range(1, amount) if counts[i] < most]
        pool, budget = sum([loads[i] for i in free]), spare
        for i in free:
            more = min(most - counts[i], max(1, budget * loads[i] // pool), spare)
            counts[i] = counts[i] + more
            spare = spare - more
    return np.array(counts)


def scatter_about(rng, extent, width, most, pieces=(), kind=jnp.bfloat16):
    result = jax.random.normal(rng, extent, jnp.float32) * width
    if len(pieces) > 0:
        result = shard_levels(rng, extent, pieces, -0.22, 0.18) * result
    return jnp.clip(result, min=-most, max=most).astype(kind)


def setup_inputs(seed: int = 0) -> dict:
    splits = jax.random.split(jax.random.key(seed), 12)
    forward_held = scatter_about(splits[0], (N_SECTION, TOKENS, D), 1.0, 6.0, ((0, 4), (1, 8)))
    forward_enter = scatter_about(splits[1], (TICKS - 1, TOKENS, D), 1.0, 6.0, ((1, 8),))
    backward_held = scatter_about(splits[2], (N_SECTION, TOKENS, D), 1.0, 6.0, ((0, 4), (1, 8)))
    backward_enter = scatter_about(splits[3], (TICKS - 1, TOKENS, D), 1.0, 6.0, ((1, 8),))
    stashed_inputs = scatter_about(splits[4], (N_SECTION, TICKS, TOKENS, D), 1.0, 6.0, ((0, 4), (2, 8)))
    gate_weight = scatter_about(splits[5], (N_SECTION, EXPERTS, D, FE), D ** -0.5, 0.09375, ((0, 4), (1, 8)))
    up_weight = scatter_about(splits[6], (N_SECTION, EXPERTS, D, FE), D ** -0.5, 0.09375, ((0, 4), (1, 8)))
    down_weight = scatter_about(splits[7], (N_SECTION, EXPERTS, FE, D), FE ** -0.5, 0.1875, ((0, 4), (1, 8)))
    norm_gain = jnp.clip(jnp.exp(math.log(2.0) - 1.3862944 * jax.random.uniform(splits[8], (N_SECTION, D), jnp.float32) ** shard_levels(splits[8], (N_SECTION, D), ((0, 4),), -0.2, 0.2)), 0.5, 2.0)
    expert_ids_keys = jax.random.split(jax.random.fold_in(splits[9], 1), N_SECTION * (2 * TICKS) * TOKENS // TOK_DEV)
    expert_ids_turns = jax.random.permutation(jax.random.fold_in(splits[9], 3), N_SECTION * (2 * TICKS) * TOKENS // TOK_DEV)
    expert_ids = jax.vmap(lambda own, number: routed_block(jax.random.fold_in(splits[9], 2), own, number, TOK_DEV, EXPERTS, TOPK, CAP, 2))(expert_ids_keys, expert_ids_turns).reshape((N_SECTION, 2 * TICKS, TOKENS, TOPK))
    router_scores = jnp.clip(jnp.exp(math.log(1.0) - 3.912023 * jax.random.uniform(splits[10], (N_SECTION, 2 * TICKS, TOKENS, TOPK), jnp.float32) ** shard_levels(splits[10], (N_SECTION, 2 * TICKS, TOKENS, TOPK), ((0, 4), (2, 8)), -0.2, 0.2)), 0.02, 1.0)
    return dict(forward_held=forward_held, forward_enter=forward_enter, backward_held=backward_held, backward_enter=backward_enter, stashed_inputs=stashed_inputs, gate_weight=gate_weight, up_weight=up_weight, down_weight=down_weight, norm_gain=norm_gain, expert_ids=expert_ids, router_scores=router_scores)


EPSILON = 1e-06
ROUTE_SCALE = 2.5

def normalized(values, gain):
    floats = values.astype(jnp.float32)
    inverse = lax.rsqrt(lax.optimization_barrier(jnp.mean(floats * floats, axis=-1, keepdims=True)) + EPSILON)
    return (floats, inverse, floats * inverse * gain)

def gate_values(scores):
    return ROUTE_SCALE * scores / lax.optimization_barrier(jnp.sum(scores, axis=-1, keepdims=True))

def forward_layer(layer_input, gain, gate_mats, up_mats, down_mats, chosen_ids, scores):
    floats, inverse, normal = normalized(layer_input, gain)
    normed = normal.astype(jnp.bfloat16)
    gates = gate_values(scores)

    def per_expert(weights):
        gate_mat, up_mat, down_mat = weights
        pre_gate = jnp.dot(normed, gate_mat, preferred_element_type=jnp.float32)
        pre_up = jnp.dot(normed, up_mat, preferred_element_type=jnp.float32)
        active = (jax.nn.silu(pre_gate) * pre_up).astype(jnp.bfloat16)
        return jnp.dot(active, down_mat, preferred_element_type=jnp.float32).astype(jnp.bfloat16)
    outputs = lax.map(per_expert, (gate_mats, up_mats, down_mats))
    token_index = jnp.arange(TOKENS, dtype=jnp.int32)[:, None]
    picked = outputs[chosen_ids, token_index].astype(jnp.float32)
    branch = lax.optimization_barrier(jnp.sum(gates[..., None] * picked, axis=1))
    return (floats + branch).astype(jnp.bfloat16)

def backward_layer(stashed, cotangent, gain, gate_mats, up_mats, down_mats, chosen_ids, scores):
    floats, inverse, normal = normalized(stashed, gain)
    normed = normal.astype(jnp.bfloat16)
    gates = gate_values(scores)
    incoming = cotangent.astype(jnp.float32)
    weighted = (gates[..., None] * incoming[:, None, :]).astype(jnp.bfloat16)

    def per_expert(total, packed):
        expert_index, gate_mat, up_mat, down_mat = packed
        chosen = (chosen_ids == expert_index)[..., None]
        slot_grad = lax.optimization_barrier(jnp.sum(jnp.where(chosen, weighted.astype(jnp.float32), jnp.float32(0.0)), axis=1)).astype(jnp.bfloat16)
        pre_gate = jnp.dot(normed, gate_mat, preferred_element_type=jnp.float32)
        pre_up = jnp.dot(normed, up_mat, preferred_element_type=jnp.float32)
        sigma = jax.nn.sigmoid(pre_gate)
        swish = pre_gate * sigma
        act_grad = jnp.dot(slot_grad, down_mat.T, preferred_element_type=jnp.float32)
        d_gate = (act_grad * pre_up * sigma * (1.0 + pre_gate * (1.0 - sigma))).astype(jnp.bfloat16)
        d_up = (act_grad * swish).astype(jnp.bfloat16)
        normed_grad = (jnp.dot(d_gate, gate_mat.T, preferred_element_type=jnp.float32) + jnp.dot(d_up, up_mat.T, preferred_element_type=jnp.float32)).astype(jnp.bfloat16)
        return (total + normed_grad.astype(jnp.float32), None)
    start = jnp.zeros((TOKENS, D), jnp.float32)
    total, unused = lax.scan(per_expert, start, (jnp.arange(EXPERTS, dtype=jnp.int32), gate_mats, up_mats, down_mats))
    combined = total * gain
    norm_term = inverse * combined - floats * inverse ** 3 * lax.optimization_barrier(jnp.mean(floats * combined, axis=-1, keepdims=True))
    return (incoming + norm_term).astype(jnp.bfloat16)

def reference(forward_held, forward_enter, backward_held, backward_enter, stashed_inputs, gate_weight, up_weight, down_weight, norm_gain, expert_ids, router_scores):
    current = forward_held
    forward_rows = []
    for tick_index in range(TICKS):
        produced = jnp.stack([forward_layer(current[section_index], norm_gain[section_index], gate_weight[section_index], up_weight[section_index], down_weight[section_index], expert_ids[section_index, tick_index], router_scores[section_index, tick_index]) for section_index in range(N_SECTION)])
        forward_rows.append(produced)
        if tick_index + 1 < TICKS:
            current = jnp.concatenate([forward_enter[tick_index][None], produced[:-1]], axis=0)
    current = backward_held
    backward_rows = []
    for tick_index in range(TICKS):
        returned = jnp.stack([backward_layer(stashed_inputs[section_index, tick_index], current[section_index], norm_gain[section_index], gate_weight[section_index], up_weight[section_index], down_weight[section_index], expert_ids[section_index, TICKS + tick_index], router_scores[section_index, TICKS + tick_index]) for section_index in range(N_SECTION)])
        backward_rows.append(returned)
        if tick_index + 1 < TICKS:
            current = jnp.concatenate([returned[1:], backward_enter[tick_index][None]], axis=0)
    return (jnp.stack(forward_rows), jnp.stack(backward_rows))
```

```python
import jax
import jax.numpy as jnp
from jax import lax
from jax.sharding import PartitionSpec as P

EXPERTS = 16
TOPK = 2
TICKS = 2
CAP = 12


EPSILON = 1e-06
ROUTE_SCALE = 2.5


def passed_along(value, axis, steps):
    count = lax.axis_size(axis)
    leading, last = (max(0, -steps), min(count, count - steps))
    return lax.ppermute(value, axis, [(source, source + steps) for source in range(leading, last)])


def normalized(values, gain):
    floats = values.astype(jnp.float32)
    inverse = lax.rsqrt(jnp.mean(floats * floats, axis=-1, keepdims=True) + EPSILON)
    return (floats, inverse, (floats * inverse * gain).astype(jnp.bfloat16))


def gate_values(scores):
    return ROUTE_SCALE * scores / jnp.sum(scores, axis=-1, keepdims=True)


def slot_table(chosen_ids, capacity, experts, local_count, me):
    flat = chosen_ids.reshape(-1)
    onehot = (flat[:, None] == jnp.arange(experts, dtype=jnp.int32)[None, :]).astype(jnp.int32)
    earlier = jnp.cumsum(onehot, axis=0) - onehot
    place = jnp.sum(earlier * onehot, axis=1)
    block = jnp.bitwise_xor(flat // local_count, me)
    return block * (local_count * capacity) + (flat % local_count) * capacity + place


def slot_selector(slots, total_slots):
    return (slots[:, None] == jnp.arange(total_slots, dtype=jnp.int32)[None, :]).astype(
        jnp.bfloat16
    )


def exchanged(parts, groups):
    size = parts[0].shape[0] // groups
    received = [[part[:size] for part in parts]]
    for k in range(1, groups):
        block = jnp.concatenate([part[k * size : (k + 1) * size] for part in parts])
        landed = lax.ppermute(block, "expert", [(i, i ^ k) for i in range(groups)])
        received.append([landed[i * size : (i + 1) * size] for i in range(len(parts))])
    return [jnp.concatenate([blocks[i] for blocks in received]) for i in range(len(parts))]


def row_masks(total_slots, local_count):
    row = jnp.arange(total_slots, dtype=jnp.int32)
    owner = (row // CAP) % local_count
    return [(owner == e)[:, None] for e in range(local_count)]


def dot(a, b, dims):
    return lax.dot_general(a, b, (dims, ((), ())), preferred_element_type=jnp.float32)


def by_row(values, masks):
    total = values[0]
    for value, mask in zip(values[1:], masks[1:]):
        total = jnp.where(mask, value, total)
    return total


def spread(value, masks):
    return jnp.concatenate([jnp.where(m, value, jnp.zeros_like(value)) for m in masks], axis=1)


def expert_forward(x, gate_local, up_local, down_local, masks):
    count = gate_local.shape[0]
    pre_gate = by_row([dot(x, gate_local[e], ((1,), (0,))) for e in range(count)], masks)
    pre_up = by_row([dot(x, up_local[e], ((1,), (0,))) for e in range(count)], masks)
    active = (jax.nn.silu(pre_gate) * pre_up).astype(jnp.bfloat16)
    down = down_local.reshape(-1, down_local.shape[-1])
    return dot(spread(active, masks), down, ((1,), (0,))).astype(jnp.bfloat16)


def expert_backward(x, grad, gate_local, up_local, down_local, masks):
    count = gate_local.shape[0]
    pre_gate = by_row([dot(x, gate_local[e], ((1,), (0,))) for e in range(count)], masks)
    pre_up = by_row([dot(x, up_local[e], ((1,), (0,))) for e in range(count)], masks)
    sigma = jax.nn.sigmoid(pre_gate)
    swish = pre_gate * sigma
    down = down_local.reshape(-1, down_local.shape[-1])
    both = dot(grad, down, ((1,), (1,)))
    hidden = down_local.shape[1]
    act_grad = by_row([both[:, e * hidden : (e + 1) * hidden] for e in range(count)], masks)
    d_gate = (act_grad * pre_up * sigma * (1.0 + pre_gate * (1.0 - sigma))).astype(jnp.bfloat16)
    d_up = (act_grad * swish).astype(jnp.bfloat16)
    sums = [
        dot(d_gate, gate_local[e], ((1,), (1,))) + dot(d_up, up_local[e], ((1,), (1,)))
        for e in range(count)
    ]
    return by_row(sums, masks).astype(jnp.bfloat16)


def local(
    forward_held,
    forward_enter,
    backward_held,
    backward_enter,
    stashed_inputs,
    gate_weight,
    up_weight,
    down_weight,
    norm_gain,
    expert_ids,
    router_scores,
):
    position = lax.axis_index("section")
    sections = lax.axis_size("section")
    me = lax.axis_index("expert")
    groups = lax.axis_size("expert")
    weights = (gate_weight[0], up_weight[0], down_weight[0])
    local_count = weights[0].shape[0]
    gain = norm_gain[0]
    rows = forward_held.shape[1]
    total_slots = EXPERTS * CAP
    masks = row_masks(total_slots, local_count)

    selects = []
    gates = []
    for j in range(2 * TICKS):
        slots = slot_table(expert_ids[0, j], CAP, EXPERTS, local_count, me)
        selects.append(slot_selector(slots, total_slots).reshape(rows, TOPK, total_slots))
        gates.append(gate_values(router_scores[0, j]))

    def dispatched(select, values):
        return dot(jnp.sum(select, axis=1), values, ((0,), (0,)))

    behind = []
    for tick in range(TICKS):
        floats, inverse, normed = normalized(stashed_inputs[0, tick], gain)
        sent = dispatched(selects[TICKS + tick], normed).astype(jnp.bfloat16)
        behind.append((floats, inverse, sent))

    def ahead_start(layer_input, tick):
        normed = normalized(layer_input, gain)[2]
        return dispatched(selects[tick], normed).astype(jnp.bfloat16)

    def ahead_end(layer_input, returned, tick):
        select = selects[tick]
        branch = sum(
            gates[tick][:, k : k + 1] * dot(select[:, k], returned, ((1,), (0,)))
            for k in range(TOPK)
        )
        return (layer_input.astype(jnp.float32) + branch).astype(jnp.bfloat16)

    def behind_start(cotangent, tick):
        select = selects[TICKS + tick]
        slot_gates = jnp.sum(
            select.astype(jnp.float32) * gates[TICKS + tick][:, :, None], axis=(0, 1)
        )
        return (slot_gates[:, None] * dispatched(select, cotangent)).astype(jnp.bfloat16)

    def behind_end(cotangent, returned, tick):
        floats, inverse, _ = behind[tick]
        tokens = jnp.sum(selects[TICKS + tick], axis=1)
        combined = dot(tokens, returned, ((1,), (0,))) * gain
        norm_term = inverse * combined - floats * inverse**3 * jnp.mean(
            floats * combined, axis=-1, keepdims=True
        )
        return (cotangent.astype(jnp.float32) + norm_term).astype(jnp.bfloat16)

    layer_input = forward_held[0]
    cotangent = backward_held[0]
    forward_rows = []
    backward_rows = []
    (behind_normed,) = exchanged([behind[0][2]], groups)
    for tick in range(TICKS):
        (behind_grad,) = exchanged([behind_start(cotangent, tick)], groups)
        (ahead_normed,) = exchanged([ahead_start(layer_input, tick)], groups)
        behind_result = expert_backward(behind_normed, behind_grad, *weights, masks)
        (behind_back,) = exchanged([behind_result], groups)
        ahead_result = expert_forward(ahead_normed, *weights, masks)
        (ahead_back,) = exchanged([ahead_result], groups)
        returned = behind_end(cotangent, behind_back, tick)
        produced = ahead_end(layer_input, ahead_back, tick)
        forward_rows.append(produced)
        backward_rows.append(returned)
        if tick + 1 < TICKS:
            (behind_normed,) = exchanged([behind[tick + 1][2]], groups)
            forward_recv = passed_along(produced, "section", 1)
            backward_recv = passed_along(returned, "section", -1)
            layer_input = jnp.where(position == 0, forward_enter[tick], forward_recv)
            cotangent = jnp.where(position == sections - 1, backward_enter[tick], backward_recv)
    return (jnp.stack(forward_rows)[:, None], jnp.stack(backward_rows)[:, None])


def solution(mesh):
    placed = (
        P("section", "expert", None),
        P(None, "expert", None),
        P("section", "expert", None),
        P(None, "expert", None),
        P("section", None, "expert", None),
        P("section", "expert", None, None),
        P("section", "expert", None, None),
        P("section", "expert", None, None),
        P("section", None),
        P("section", None, "expert", None),
        P("section", None, "expert", None),
    )
    return jax.shard_map(
        local,
        mesh=mesh,
        in_specs=placed,
        out_specs=(P(None, "section", "expert", None), P(None, "section", "expert", None)),
        check_vma=False,
    )
```
